32 devices in a mesh: gx: 4 (over z), gy: 8 (over y, x, core).
Axes of the slice: x: 2, y: 2, z: 4, core: 2. Of those that a mesh axis runs over, the one named last changes fastest.
Arguments:
- saved_pops: bfloat16 [4, 19, 64, 4096], P(None, None, 'gx', 'gy'), may hold values from 0.099609375 to 1.8984375
- seed_adjoint: float32 [19, 64, 4096], P(None, 'gx', 'gy'), may hold values from -6 to 6
- solid_label: int32 [64, 4096], P('gx', 'gy'), may hold values 0 or 1
- design_mask: int32 [64, 4096], P('gx', 'gy'), may hold values 0 or 1
- design_field: float32 [64, 4096], P('gx', 'gy'), may hold values from 0 to 1
Outputs:
- adjoint_out: float32 [19, 64, 4096], P(None, 'gx', 'gy')
- sensitivity: float32 [64, 4096], P('gx', 'gy')
The draws below stay inside these ranges and needn't reach their ends.
All inputs are finite; a program needn't handle non-finite values. No bound on the sum of `solid_label` or of `design_mask` on one device may be relied on, other than what follows from the above.
Results may differ from the reference program's by a relative error of at most 0.0003.
Values sent between devices are 32-bit elements; how exact they have to be, the bound alone decides.
A program may use at most 64 MiB of HBM per device.

```python
import jax
import jax.numpy as jnp
import numpy as np
from jax import lax

CX = 16
NZ = 32
STEPS = 4
NX = 64
NY = 128
N_GX = 4


def set_ends(values, own_key, low, top_value):
    longest = values.shape.index(max(values.shape))
    spots = []
    for shift in (0, 1):
        where = [jax.random.randint(jax.random.fold_in(own_key, axis), (), 0, length) for axis, length in enumerate(values.shape)]
        where[longest] = (where[longest] + shift) % values.shape[longest]
        spots.append(tuple(where))
    return values.at[spots[0]].set(low).at[spots[1]].set(top_value)


def block_levels(rng, shape, pieces, low, top_value):
    loudness = 1.0
    for axis_at, shards_of in pieces:
        heights = jax.random.uniform(jax.random.fold_in(jax.random.fold_in(rng, 6), axis_at), (shards_of,), jnp.float32, low / len(pieces), top_value / len(pieces))
        loudness = loudness * jnp.repeat(jnp.exp(heights), shape[axis_at] // shards_of).reshape((-1,) + (1,) * (len(shape) - 1 - axis_at))
    return loudness


def normal_values(key, extent, spread, bound, cuts=(), held_as=jnp.bfloat16):
    values = spread * jax.random.normal(key, extent, jnp.float32)
    if cuts:
        values = values * block_levels(key, extent, cuts, -0.22, 0.18)
    return jnp.clip(values, -bound, bound).astype(held_as)


def setup_inputs(seed: int = 0) -> dict:
    arg_keys = jax.random.split(jax.random.key(seed), 6)
    saved_pops = jnp.clip(1.0 + 0.18 * jax.random.normal(arg_keys[0], (STEPS, 19, NX, NY * NZ), jnp.float32), 0.099609375, 1.8984375).astype(jnp.bfloat16)
    seed_adjoint = normal_values(arg_keys[1], (19, NX, NY * NZ), 1.0, 6.0, ((1, 4), (2, 8)), jnp.float32)
    solid_label = set_ends((jax.random.randint(arg_keys[2], (NX, NY * NZ), 0, 4) < 1).astype(jnp.int32), jax.random.fold_in(arg_keys[2], 1), 0, 1)
    design_mask = set_ends((jax.random.randint(arg_keys[3], (NX, NY * NZ), 0, 2) < 1).astype(jnp.int32), jax.random.fold_in(arg_keys[3], 1), 0, 1)
    design_field = jnp.clip(1.0 * jax.random.uniform(arg_keys[4], (NX, NY * NZ), jnp.float32) ** block_levels(arg_keys[4], (NX, NY * NZ), ((0, 4), (1, 8)), -0.2, 0.2), 0.0, 1.0)
    return dict(saved_pops=saved_pops, seed_adjoint=seed_adjoint, solid_label=solid_label, design_mask=design_mask, design_field=design_field)


VELOCITIES = np.array([[0, 0, 0], [1, 0, 0], [-1, 0, 0], [0, 1, 0], [0, -1, 0], [0, 0, 1], [0, 0, -1], [1, 1, 0], [1, -1, 0], [-1, 1, 0], [-1, -1, 0], [1, 0, 1], [1, 0, -1], [-1, 0, 1], [-1, 0, -1], [0, 1, 1], [0, 1, -1], [0, -1, 1], [0, -1, -1]])
LATTICE_WEIGHTS = np.array([1.0 / 3.0] + [1.0 / 18.0] * 6 + [1.0 / 36.0] * 12)
OPPOSITE = np.array([0, 2, 1, 4, 3, 6, 5, 10, 9, 8, 7, 14, 13, 12, 11, 18, 17, 16, 15])
OMEGA_BASE = 1.0
OMEGA_SPAN = 0.8
SENS_SCALE = 10.0

def collide(pops, rates, solid):
    density = lax.optimization_barrier(jnp.sum(pops, axis=0))
    velo = jnp.asarray(VELOCITIES, jnp.float32)
    momentum = jnp.tensordot(velo.T, pops, axes=1, precision=lax.Precision.HIGHEST)
    speed = momentum / density
    projected = jnp.tensordot(velo, speed, axes=1, precision=lax.Precision.HIGHEST)
    speed_sq = lax.optimization_barrier(jnp.sum(speed * speed, axis=0))
    weights = jnp.asarray(LATTICE_WEIGHTS, jnp.float32).reshape((19,) + (1,) * (pops.ndim - 1))
    equilibrium = weights * density * (1.0 + 3.0 * projected + 4.5 * projected * projected - 1.5 * speed_sq)
    fluid = pops - rates * (pops - equilibrium)
    bounce = pops[OPPOSITE]
    return jnp.where(solid > 0, bounce, fluid)

def adjoint_block(args):
    pops, pulled, rates, solid = args

    def local(values, rate_values):
        return collide(values, rate_values, solid)
    unused, backward = jax.vjp(local, pops, rates)
    return backward(pulled)

def reference(saved_pops, seed_adjoint, solid_label, design_mask, design_field):
    mask_float = design_mask.astype(jnp.float32)
    rates = OMEGA_BASE + OMEGA_SPAN * design_field * mask_float
    weights = jnp.asarray(LATTICE_WEIGHTS, jnp.float32).reshape(19, 1, 1)
    flat = NY * NZ
    adjoint = seed_adjoint
    sensitivity = jnp.zeros((NX, flat), jnp.float32)

    def blocks(array):
        lead = array.shape[:-2]
        moved = array.reshape(lead + (N_GX, CX, flat))
        return jnp.moveaxis(moved, len(lead), 0)

    def unblock(array):
        lead = array.shape[1:-2]
        moved = jnp.moveaxis(array, 0, len(lead))
        return moved.reshape(lead + (NX, flat))
    for step in reversed(range(STEPS)):
        cube = adjoint.reshape(19, NX, NY, NZ)
        pulled = jnp.stack([jnp.roll(cube[k], (-int(VELOCITIES[k, 0]), -int(VELOCITIES[k, 1]), -int(VELOCITIES[k, 2])), (0, 1, 2)) for k in range(19)])
        pulled = pulled.reshape(19, NX, flat)
        pops = saved_pops[step].astype(jnp.float32) * weights
        new_adj, rate_bar = lax.map(adjoint_block, (blocks(pops), blocks(pulled), blocks(rates), blocks(solid_label)))
        adjoint = unblock(new_adj)
        sensitivity = sensitivity + SENS_SCALE * OMEGA_SPAN * mask_float * unblock(rate_bar)
    return (adjoint, sensitivity)
```

```python
import functools

import jax
import jax.numpy as jnp
import numpy as np
from jax import lax
from jax.experimental import pallas as pl
from jax.experimental.pallas import tpu as pltpu
from jax.sharding import PartitionSpec as P

NZ = 32
LANES = 128
MESH = pl.DeviceIdType.MESH

VELOCITIES = [
    (0, 0, 0),
    (1, 0, 0), (-1, 0, 0), (0, 1, 0), (0, -1, 0), (0, 0, 1), (0, 0, -1),
    (1, 1, 0), (1, -1, 0), (-1, 1, 0), (-1, -1, 0),
    (1, 0, 1), (1, 0, -1), (-1, 0, 1), (-1, 0, -1),
    (0, 1, 1), (0, 1, -1), (0, -1, 1), (0, -1, -1),
]
OPPOSITE = [0, 2, 1, 4, 3, 6, 5, 10, 9, 8, 7, 14, 13, 12, 11, 18, 17, 16, 15]
OMEGA_BASE = 1.0
OMEGA_SPAN = 0.8
SENS_SCALE = 10.0

ORDER = [1, 7, 8, 11, 12, 2, 9, 10, 13, 14, 0, 3, 4, 5, 6, 15, 16, 17, 18]
PLACE = [ORDER.index(k) for k in range(19)]
PACKED = {
    3: (0, 0, 0), 7: (0, 0, 1), 9: (0, 0, 2), 15: (0, 0, 3), 16: (0, 1, 0),
    4: (1, 0, 3), 8: (1, 0, 2), 10: (1, 0, 1), 17: (1, 0, 0), 18: (1, 1, 3),
}
TOP = 8


def roll_lanes(value, shift):
    shift = shift % LANES
    return value if shift == 0 else pltpu.roll(value, shift, 1)


def kernel(
    num_x, num_y, steps, width, flat,
    saved_hbm, seed_hbm, solid_hbm, mask_hbm, field_hbm,
    out_hbm, sens_hbm,
    saved, seed, solid_ref, mask_ref, field_ref,
    adj, ysend, yrecv, flow, rate_ref, out, sens,
    in_sem, saved_sem, out_sem, send_sem, recv_sem,
):
    tiles = flat // LANES
    gx, gy = lax.axis_index("gx"), lax.axis_index("gy")
    west, east = lax.rem(gx + num_x - 1, num_x), lax.rem(gx + 1, num_x)
    south, north = lax.rem(gy + num_y - 1, num_y), lax.rem(gy + 1, num_y)

    barrier = pltpu.get_barrier_semaphore()
    around = [
        (west, gy), (east, gy), (gx, south), (gx, north),
        (west, south), (east, south), (west, north), (east, north),
    ]
    loads = [
        pltpu.make_async_copy(seed_hbm, seed, in_sem.at[0]),
        pltpu.make_async_copy(solid_hbm, solid_ref, in_sem.at[1]),
        pltpu.make_async_copy(mask_hbm, mask_ref, in_sem.at[2]),
        pltpu.make_async_copy(field_hbm, field_ref, in_sem.at[3]),
    ]
    saved_loads = [
        pltpu.make_async_copy(saved_hbm.at[s], saved.at[s], saved_sem.at[s]) for s in range(steps)
    ]
    loads[0].start()
    for device in around:
        pl.semaphore_signal(barrier, inc=1, device_id=device, device_id_type=MESH)
    for load in loads[1:]:
        load.start()
    for s in reversed(range(steps)):
        saved_loads[s].start()

    lane = lax.broadcasted_iota(jnp.int32, (width, LANES), 1)
    depth = lane % NZ
    own = pl.ds(TOP, width)

    def transfers(n):
        moves = []

        def add(src, dst, device):
            i = len(moves)
            moves.append(
                pltpu.make_async_remote_copy(
                    src_ref=src, dst_ref=dst,
                    send_sem=send_sem.at[n, i], recv_sem=recv_sem.at[n, i],
                    device_id=device, device_id_type=MESH,
                )
            )

        rows = {1: (TOP, TOP + width), -1: (TOP + width - 1, TOP - 1)}
        for first, step_x, device in ((0, 1, (west, gy)), (5, -1, (east, gy))):
            src_row, dst_row = rows[step_x]
            group = adj.at[n, pl.ds(first, 5)]
            add(group.at[:, :, pl.ds(src_row, 1)], group.at[:, :, pl.ds(dst_row, 1)], device)
        for side, device in ((0, (gx, south)), (1, (gx, north))):
            add(ysend.at[n, side, :, own], yrecv.at[n, side, :, own], device)
        for side, step_x, device in (
            (0, 1, (west, south)), (0, -1, (east, south)), (1, 1, (west, north)), (1, -1, (east, north)),
        ):
            src_row, dst_row = rows[step_x]
            add(
                ysend.at[n, side, 0, pl.ds(src_row, 1)],
                yrecv.at[n, side, 0, pl.ds(dst_row, 1)],
                device,
            )
        return moves

    def pack(n, side, value):
        blocks, extra = [None] * 4, None
        for k, (where, tile, block) in PACKED.items():
            if where != side:
                continue
            if tile == 1:
                extra = value(k)
            else:
                blocks[block] = roll_lanes(value(k), NZ * (block - (0 if side == 0 else 3)))
        low = jnp.where(lane < NZ, blocks[0], blocks[1])
        high = jnp.where(lane < 3 * NZ, blocks[2], blocks[3])
        ysend[n, side, 0, own, :] = jnp.where(lane < 2 * NZ, low, high)
        ysend[n, side, 1, own, :] = extra

    def pulled_tile(n, k, t):
        step_x, step_y, step_z = VELOCITIES[k]
        rows = pl.ds(TOP + step_x, width)
        value = adj[n, PLACE[k], t, rows, :]
        if step_y != 0:
            other = t + step_y
            if 0 <= other < tiles:
                beside = adj[n, PLACE[k], other, rows, :]
            else:
                side, tile, block = PACKED[k]
                beside = roll_lanes(
                    yrecv[n, side, tile, rows, :], NZ * ((0 if side == 0 else 3) - block)
                )
            edge = lane < NZ if step_y == 1 else lane >= LANES - NZ
            value = jnp.where(edge, beside, value)
        shift = -NZ * step_y
        if step_z == 0:
            return roll_lanes(value, shift)
        wraps = depth == (NZ - 1 if step_z == 1 else 0)
        return jnp.where(
            wraps,
            roll_lanes(value, shift - step_z + NZ * step_z),
            roll_lanes(value, shift - step_z),
        )

    def moments(v):
        xy_a, xy_b, xy_c, xy_d = v(7) + v(8), v(9) + v(10), v(7) - v(8), v(9) - v(10)
        xz_a, xz_b, xz_c, xz_d = v(11) + v(12), v(13) + v(14), v(11) - v(12), v(13) - v(14)
        yz_a, yz_b, yz_c, yz_d = v(15) + v(16), v(17) + v(18), v(15) - v(16), v(17) - v(18)
        xy, xz, yz = xy_a + xy_b, xz_a + xz_b, yz_a + yz_b
        face_x, face_y, face_z = 2.0 * (v(1) + v(2)), 2.0 * (v(3) + v(4)), 2.0 * (v(5) + v(6))
        total = 12.0 * v(0) + (face_x + face_y + face_z) + (xy + xz + yz)
        first = (
            2.0 * (v(1) - v(2)) + (xy_a - xy_b) + (xz_a - xz_b),
            2.0 * (v(3) - v(4)) + (xy_c + xy_d) + (yz_a - yz_b),
            2.0 * (v(5) - v(6)) + (xz_c + xz_d) + (yz_c + yz_d),
        )
        second = (
            face_x + xy + xz, face_y + xy + yz, face_z + xz + yz,
            xy_c - xy_d, xz_c - xz_d, yz_c - yz_d,
        )
        return total, first, second

    def prepare(s):
        for t in range(tiles):
            cols = pl.ds(t * LANES, LANES)
            pops = [saved[s, k, :, cols].astype(jnp.float32) for k in range(19)]
            total, first, unused = moments(lambda k: pops[k])
            inverse = 1.0 / total
            flow[s, 0, t] = total
            for axis in range(3):
                flow[s, 1 + axis, t] = first[axis] * inverse

    def advance(n, t, emit):
        s = steps - 1 - n
        cols = pl.ds(t * LANES, LANES)
        p = [pulled_tile(n, k, t) for k in range(19)]
        total, first, second = moments(lambda k: p[k])
        density, ux, uy, uz = (flow[s, i, t] for i in range(4))
        xx, yy, zz, xy, xz, yz = (0.25 * value for value in second)
        gx_, gy_, gz_ = (value * (1.0 / 12.0) for value in first)
        total3 = total * (1.0 / 12.0)
        dx = gx_ + (xx - total3) * ux + xy * uy + xz * uz
        dy = gy_ + (yy - total3) * uy + xy * ux + yz * uz
        dz = gz_ + (zz - total3) * uz + xz * ux + yz * uy
        half_g = 0.5 * (gx_ * ux + gy_ * uy + gz_ * uz)
        half_d = 0.5 * (dx * ux + dy * uy + dz * uz)
        base = total * (1.0 / 36.0) + half_g
        prod = [p[k] * saved[s, k, :, cols].astype(jnp.float32) for k in range(19)]
        faces = (prod[1] + prod[2]) + (prod[3] + prod[4]) + (prod[5] + prod[6])
        edges = ((prod[7] + prod[8]) + (prod[9] + prod[10])) + ((prod[11] + prod[12]) + (prod[13] + prod[14]))
        edges = edges + ((prod[15] + prod[16]) + (prod[17] + prod[18]))
        gain = density * (base + half_d) - (12.0 * prod[0] + 2.0 * faces + edges)
        sens_now = gain if n == 0 else sens[:, cols] + gain
        solid = solid_ref[:, cols] > 0
        if n == steps - 1:
            factor = mask_ref[:, cols].astype(jnp.float32) * (SENS_SCALE * OMEGA_SPAN / 36.0)
            sens_now = jnp.where(solid, 0.0, factor * sens_now)
        sens[:, cols] = sens_now
        rate = rate_ref[:, cols]
        keep = 1.0 - rate
        base = rate * (base - half_d)
        dx, dy, dz = rate * dx, rate * dy, rate * dz
        px, mx = base + dx, base - dx
        py, my = base + dy, base - dy
        terms = {
            (0, 0, 0): base,
            (1, 0, 0): px, (-1, 0, 0): mx, (0, 1, 0): py, (0, -1, 0): my,
            (0, 0, 1): base + dz, (0, 0, -1): base - dz,
            (1, 1, 0): px + dy, (1, -1, 0): px - dy, (-1, 1, 0): mx + dy, (-1, -1, 0): mx - dy,
            (1, 0, 1): px + dz, (1, 0, -1): px - dz, (-1, 0, 1): mx + dz, (-1, 0, -1): mx - dz,
            (0, 1, 1): py + dz, (0, 1, -1): py - dz, (0, -1, 1): my + dz, (0, -1, -1): my - dz,
        }
        fresh = []
        for k in range(19):
            value = jnp.where(solid, p[OPPOSITE[k]], keep * p[k] + terms[VELOCITIES[k]])
            fresh.append(value)
            emit(k, value)
        return fresh

    loads[0].wait()
    for k in ORDER:
        for t in range(tiles):
            adj[0, PLACE[k], t, own, :] = seed[k, :, pl.ds(t * LANES, LANES)]
    pack(0, 0, lambda k: seed[k, :, pl.ds(0, LANES)])
    pack(0, 1, lambda k: seed[k, :, pl.ds((tiles - 1) * LANES, LANES)])
    pl.semaphore_wait(barrier, 8)
    moves = transfers(0)
    for move in moves:
        move.start()

    for load in loads[1:]:
        load.wait()
    for t in range(tiles):
        cols = pl.ds(t * LANES, LANES)
        rate_ref[:, cols] = (
            OMEGA_BASE + OMEGA_SPAN * field_ref[:, cols] * mask_ref[:, cols].astype(jnp.float32)
        )
    sent = []
    stores = []
    for n in range(steps):
        s = steps - 1 - n
        saved_loads[s].wait()
        prepare(s)
        for move in moves:
            move.wait_recv()
        sent += moves
        last = n == steps - 1
        edge_tiles = [0] if tiles == 1 else [0, tiles - 1]
        for t in edge_tiles + list(range(1, tiles - 1)):
            cols = pl.ds(t * LANES, LANES)
            if last:
                def emit(k, value):
                    out[k, :, cols] = value
            else:
                def emit(k, value):
                    adj[n + 1, PLACE[k], t, own, :] = value
            fresh = advance(n, t, emit)
            if last:
                store = pltpu.make_async_copy(out.at[:, :, cols], out_hbm.at[:, :, cols], out_sem.at[t])
                store.start()
                stores.append(store)
                continue
            if t == 0:
                pack(n + 1, 0, lambda k: fresh[k])
            if t == tiles - 1:
                pack(n + 1, 1, lambda k: fresh[k])
            if t == edge_tiles[-1]:
                moves = transfers(n + 1)
                for move in moves[2:]:
                    move.start()
        if not last:
            for move in moves[:2]:
                move.start()
    store = pltpu.make_async_copy(sens, sens_hbm, out_sem.at[tiles])
    store.start()
    stores.append(store)
    for move in sent:
        move.wait_send()
    for store in stores:
        store.wait()


def solution(mesh):
    num_x, num_y = mesh.shape["gx"], mesh.shape["gy"]

    def body(saved_pops, seed_adjoint, solid_label, design_mask, design_field):
        steps = saved_pops.shape[0]
        width, flat = seed_adjoint.shape[1:]
        tiles = flat // LANES
        rows = 2 * TOP + width
        f32 = jnp.float32
        whole = pl.BlockSpec(memory_space=pl.ANY)
        return pl.pallas_call(
            functools.partial(kernel, num_x, num_y, steps, width, flat),
            out_shape=(
                jax.ShapeDtypeStruct((19, width, flat), f32),
                jax.ShapeDtypeStruct((width, flat), f32),
            ),
            in_specs=[whole] * 5,
            out_specs=(whole, whole),
            scratch_shapes=[
                pltpu.VMEM((steps, 19, width, flat), saved_pops.dtype),
                pltpu.VMEM((19, width, flat), f32),
                pltpu.VMEM((width, flat), jnp.int32),
                pltpu.VMEM((width, flat), jnp.int32),
                pltpu.VMEM((width, flat), f32),
                pltpu.VMEM((steps, 19, tiles, rows, LANES), f32),
                pltpu.VMEM((steps, 2, 2, rows, LANES), f32),
                pltpu.VMEM((steps, 2, 2, rows, LANES), f32),
                pltpu.VMEM((steps, 4, tiles, width, LANES), f32),
                pltpu.VMEM((width, flat), f32),
                pltpu.VMEM((19, width, flat), f32),
                pltpu.VMEM((width, flat), f32),
                pltpu.SemaphoreType.DMA((4,)),
                pltpu.SemaphoreType.DMA((steps,)),
                pltpu.SemaphoreType.DMA((tiles + 1,)),
                pltpu.SemaphoreType.DMA((steps, 8)),
                pltpu.SemaphoreType.DMA((steps, 8)),
            ],
            compiler_params=pltpu.CompilerParams(
                collective_id=0, has_side_effects=True, vmem_limit_bytes=40 * 1024 * 1024
            ),
        )(saved_pops, seed_adjoint, solid_label, design_mask, design_field)

    in_specs = (
        P(None, None, "gx", "gy"),
        P(None, "gx", "gy"),
        P("gx", "gy"),
        P("gx", "gy"),
        P("gx", "gy"),
    )
    out_specs = (P(None, "gx", "gy"), P("gx", "gy"))
    return jax.shard_map(body, mesh=mesh, in_specs=in_specs, out_specs=out_specs, check_vma=False)
```

```python
import functools

import jax
import jax.numpy as jnp
import numpy as np
from jax import lax
from jax.experimental import pallas as pl
from jax.experimental.pallas import tpu as pltpu
from jax.sharding import PartitionSpec as P

NZ = 32
LANES = 128
MESH = pl.DeviceIdType.MESH

VELOCITIES = [
    (0, 0, 0),
    (1, 0, 0), (-1, 0, 0), (0, 1, 0), (0, -1, 0), (0, 0, 1), (0, 0, -1),
    (1, 1, 0), (1, -1, 0), (-1, 1, 0), (-1, -1, 0),
    (1, 0, 1), (1, 0, -1), (-1, 0, 1), (-1, 0, -1),
    (0, 1, 1), (0, 1, -1), (0, -1, 1), (0, -1, -1),
]
OPPOSITE = [0, 2, 1, 4, 3, 6, 5, 10, 9, 8, 7, 14, 13, 12, 11, 18, 17, 16, 15]
OMEGA_BASE = 1.0
OMEGA_SPAN = 0.8
SENS_SCALE = 10.0

EXTRA_ROWS = 8
WIDTH_SENT = 2


def roll_lanes(value, shift):
    shift = shift % LANES
    return value if shift == 0 else pltpu.roll(value, shift, 1)


def kernel(
    num_x, num_y, steps, width, flat,
    saved_hbm, seed_hbm, solid_hbm, mask_hbm, field_hbm,
    out_hbm, sens_hbm,
    saved, solid_ref, mask_ref, field_ref,
    adj, xsend, xrecv, ysend, yrecv, density_ref, speed, mark, out, sens,
    in_sem, seed_sem, saved_sem, out_sem, send_sem, recv_sem,
):
    tiles = flat // LANES
    ring = width + EXTRA_ROWS
    half = LANES // 2
    gx, gy = lax.axis_index("gx"), lax.axis_index("gy")
    west, east = lax.rem(gx + num_x - 1, num_x), lax.rem(gx + 1, num_x)
    south, north = lax.rem(gy + num_y - 1, num_y), lax.rem(gy + 1, num_y)

    barrier = pltpu.get_barrier_semaphore()
    around = [
        (west, south), (east, south), (west, north), (east, north),
        (west, gy), (east, gy), (gx, south), (gx, north),
    ]
    for device in around:
        pl.semaphore_signal(barrier, inc=1, device_id=device, device_id_type=MESH)
    own = pl.ds(0, width)

    def columns(t):
        return pl.ds(t * LANES, LANES)

    loads = [
        pltpu.make_async_copy(solid_hbm, solid_ref, in_sem.at[0]),
        pltpu.make_async_copy(mask_hbm, mask_ref, in_sem.at[1]),
        pltpu.make_async_copy(field_hbm, field_ref, in_sem.at[2]),
    ]
    seed_loads = [
        pltpu.make_async_copy(seed_hbm.at[:, :, columns(t)], adj.at[0, :, t, own], seed_sem.at[t])
        for t in range(tiles)
    ]
    saved_loads = [
        pltpu.make_async_copy(saved_hbm.at[steps - 1 - n], saved.at[steps - 1 - n], saved_sem.at[n])
        for n in range(steps)
    ]
    ahead = list(range(0, steps, 2))
    for n in ahead:
        saved_loads[n].start()
    for load in loads + seed_loads:
        load.start()
    for n in range(1, steps, 2):
        saved_loads[n].start()

    lane = lax.broadcasted_iota(jnp.int32, (ring, LANES), 1)
    depth = lane % NZ

    def view(n, item):
        if isinstance(item, int):
            return adj.at[n, item]
        return mark.at[item[1]] if item[0] == "mark" else speed.at[item[1], item[2]]

    def plan(n):
        fields = []
        if n == 0:
            fields = [("speed", m, axis) for m in ahead if m + 1 < steps for axis in range(3)]
            fields += [("mark", 0), ("mark", 1)]
        rows, packs = [], []
        for sign in (1, -1):
            near, next_one = (0, 1) if sign == 1 else (width - 1, width - 2)
            rows.append(
                [(k, near) for k in range(19) if VELOCITIES[k][0] * sign >= 0]
                + [(k, next_one) for k in range(19) if VELOCITIES[k][0] * sign > 0]
                + [(field, near) for field in fields]
            )
            packs.append([k for k in range(19) if VELOCITIES[k][1] * sign >= 0] + fields)
        return rows, packs

    def place(row):
        return width + row if row < WIDTH_SENT else ring - width + row

    def transfers(n):
        pair = n // 2
        rows, packs = plan(n)
        moves = []

        def add(src, dst, device):
            i = len(moves)
            moves.append(
                pltpu.make_async_remote_copy(
                    src_ref=src, dst_ref=dst,
                    send_sem=send_sem.at[pair, i], recv_sem=recv_sem.at[pair, i],
                    device_id=device, device_id_type=MESH,
                )
            )

        for side, by_x in ((0, (west, east)), (1, (west, east))):
            by_y = (south, north)[side]
            count = pl.ds(0, (len(packs[side]) + 1) // 2)
            for x, src_row, dst_row in (
                (by_x[0], 0, width), (by_x[1], width - WIDTH_SENT, ring - WIDTH_SENT),
            ):
                add(
                    ysend.at[pair, side, count, pl.ds(src_row, WIDTH_SENT)],
                    yrecv.at[pair, side, count, pl.ds(dst_row, WIDTH_SENT)],
                    (x, by_y),
                )
        for side, by_y in ((0, south), (1, north)):
            count = pl.ds(0, (len(packs[side]) + 1) // 2)
            add(ysend.at[pair, side, count, own], yrecv.at[pair, side, count, own], (gx, by_y))
        for side, by_x in ((0, west), (1, east)):
            count = pl.ds(0, len(rows[side]) * tiles)
            add(xsend.at[pair, side, count], xrecv.at[pair, side, count], (by_x, gy))
        return moves

    def first_half(side):
        return (lane < half) if side == 0 else (lane >= half)

    def pack_y(n, side):
        pack = plan(n)[1][side]
        t = 0 if side == 0 else tiles - 1
        for i in range(0, len(pack), 2):
            value = view(n, pack[i])[t, own, :]
            if i + 1 < len(pack):
                second = roll_lanes(view(n, pack[i + 1])[t, own, :], half)
                value = jnp.where(first_half(side)[:width], value, second)
            ysend[n // 2, side, i // 2, own, :] = value

    def pack_x(n):
        for side, rows in enumerate(plan(n)[0]):
            for j, (item, row) in enumerate(rows):
                for t in range(tiles):
                    xsend[n // 2, side, pl.ds(j * tiles + t, 1), :] = view(n, item)[t, pl.ds(row, 1), :]

    def unpack(n):
        rows, packs = plan(n)
        for side in range(2):
            for j, (item, row) in enumerate(rows[side]):
                for t in range(tiles):
                    view(n, item)[t, pl.ds(place(row), 1), :] = xrecv[
                        n // 2, side, pl.ds(j * tiles + t, 1), :
                    ]

        def arrived(side, item):
            if item not in packs[side]:
                return None
            i = packs[side].index(item)
            return roll_lanes(yrecv[n // 2, side, i // 2], half * (i % 2))

        for item in packs[0] + [item for item in packs[1] if item not in packs[0]]:
            after, before = arrived(0, item), arrived(1, item)
            if after is None or before is None:
                value = before if after is None else after
            else:
                value = jnp.where(lane < half, after, before)
            view(n, item)[tiles] = value

    def pulled_tile(n, k, t, count):
        step_x, step_y, step_z = VELOCITIES[k]
        if step_x == 0:
            rows = pl.ds(0, count)
        elif step_x == 1 and count == width:
            rows, step_x = pl.ds(1, count), 0
        else:
            rows = pl.ds(0, ring)
        value = adj[n, k, t, rows, :]
        if step_y != 0:
            beside = adj[n, k, (t + step_y) % (tiles + 1), rows, :]
            at = lane[: value.shape[0]]
            value = jnp.where(at < NZ if step_y == 1 else at >= LANES - NZ, beside, value)
        if step_x != 0:
            value = pltpu.roll(value, (-step_x) % ring, 0)[:count]
        shift = -NZ * step_y
        if step_z == 0:
            return roll_lanes(value, shift)
        return jnp.where(
            depth[:count] == (NZ - 1 if step_z == 1 else 0),
            roll_lanes(value, shift - step_z + NZ * step_z),
            roll_lanes(value, shift - step_z),
        )

    def moments(v):
        xy_a, xy_b, xy_c, xy_d = v(7) + v(8), v(9) + v(10), v(7) - v(8), v(9) - v(10)
        xz_a, xz_b, xz_c, xz_d = v(11) + v(12), v(13) + v(14), v(11) - v(12), v(13) - v(14)
        yz_a, yz_b, yz_c, yz_d = v(15) + v(16), v(17) + v(18), v(15) - v(16), v(17) - v(18)
        xy, xz, yz = xy_a + xy_b, xz_a + xz_b, yz_a + yz_b
        face_x, face_y, face_z = 2.0 * (v(1) + v(2)), 2.0 * (v(3) + v(4)), 2.0 * (v(5) + v(6))
        total = 12.0 * v(0) + (face_x + face_y + face_z) + (xy + xz + yz)
        first = (
            2.0 * (v(1) - v(2)) + (xy_a - xy_b) + (xz_a - xz_b),
            2.0 * (v(3) - v(4)) + (xy_c + xy_d) + (yz_a - yz_b),
            2.0 * (v(5) - v(6)) + (xz_c + xz_d) + (yz_c + yz_d),
        )
        second = (
            face_x + xy + xz, face_y + xy + yz, face_z + xz + yz,
            xy_c - xy_d, xz_c - xz_d, yz_c - yz_d,
        )
        return total, first, second

    def prepare(n):
        saved_loads[n].wait()
        for t in range(tiles):
            pops = [saved[steps - 1 - n, k, :, columns(t)].astype(jnp.float32) for k in range(19)]
            total, first, unused = moments(lambda k: pops[k])
            inverse = 1.0 / total
            density_ref[n, t] = total
            for axis in range(3):
                speed[n, axis, t, own, :] = first[axis] * inverse

    def advance(n, t, count, emit):
        s = steps - 1 - n
        cols = columns(t)
        rows = pl.ds(0, count)
        p = [pulled_tile(n, k, t, count) for k in range(19)]
        total, first, second = moments(lambda k: p[k])
        ux, uy, uz = (speed[n, axis, t, rows, :] for axis in range(3))
        xx, yy, zz, xy, xz, yz = (0.25 * value for value in second)
        gx_, gy_, gz_ = (value * (1.0 / 12.0) for value in first)
        total3 = total * (1.0 / 12.0)
        dx = gx_ + (xx - total3) * ux + xy * uy + xz * uz
        dy = gy_ + (yy - total3) * uy + xy * ux + yz * uz
        dz = gz_ + (zz - total3) * uz + xz * ux + yz * uy
        half_g = 0.5 * (gx_ * ux + gy_ * uy + gz_ * uz)
        half_d = 0.5 * (dx * ux + dy * uy + dz * uz)
        base = total * (1.0 / 36.0) + half_g
        solid = mark[1, t, rows, :] > 0.5
        if t < tiles:
            prod = [p[k][:width] * saved[s, k, :, cols].astype(jnp.float32) for k in range(19)]
            faces = (prod[1] + prod[2]) + (prod[3] + prod[4]) + (prod[5] + prod[6])
            edges = ((prod[7] + prod[8]) + (prod[9] + prod[10])) + (
                (prod[11] + prod[12]) + (prod[13] + prod[14])
            )
            edges = edges + ((prod[15] + prod[16]) + (prod[17] + prod[18]))
            gain = density_ref[n, t] * (base + half_d)[:width] - (12.0 * prod[0] + 2.0 * faces + edges)
            sens_now = gain if n == 0 else sens[:, cols] + gain
            if n == steps - 1:
                factor = mask_ref[:, cols].astype(jnp.float32) * (SENS_SCALE * OMEGA_SPAN / 36.0)
                sens_now = jnp.where(solid[:width], 0.0, factor * sens_now)
            sens[:, cols] = sens_now
        rate = mark[0, t, rows, :]
        keep = 1.0 - rate
        base = rate * (base - half_d)
        dx, dy, dz = rate * dx, rate * dy, rate * dz
        px, mx = base + dx, base - dx
        py, my = base + dy, base - dy
        terms = {
            (0, 0, 0): base,
            (1, 0, 0): px, (-1, 0, 0): mx, (0, 1, 0): py, (0, -1, 0): my,
            (0, 0, 1): base + dz, (0, 0, -1): base - dz,
            (1, 1, 0): px + dy, (1, -1, 0): px - dy, (-1, 1, 0): mx + dy, (-1, -1, 0): mx - dy,
            (1, 0, 1): px + dz, (1, 0, -1): px - dz, (-1, 0, 1): mx + dz, (-1, 0, -1): mx - dz,
            (0, 1, 1): py + dz, (0, 1, -1): py - dz, (0, -1, 1): my + dz, (0, -1, -1): my - dz,
        }
        for k in range(19):
            if t == tiles and VELOCITIES[k][1] == 0:
                continue
            some = count if VELOCITIES[k][0] != 0 else width
            emit(
                k, some,
                jnp.where(
                    solid[:some], p[OPPOSITE[k]][:some],
                    keep[:some] * p[k][:some] + terms[VELOCITIES[k]][:some],
                ),
            )

    for load in loads:
        load.wait()
    for t in range(tiles):
        cols = columns(t)
        mark[0, t, own, :] = (
            OMEGA_BASE + OMEGA_SPAN * field_ref[:, cols] * mask_ref[:, cols].astype(jnp.float32)
        )
        mark[1, t, own, :] = (solid_ref[:, cols] > 0).astype(jnp.float32)
    for n in ahead:
        prepare(n)
    for load in seed_loads:
        load.wait()

    sent, stores = [], []
    for n in range(steps):
        if n % 2 == 0:
            for side in range(2):
                pack_y(n, side)
            if n == 0:
                pl.semaphore_wait(barrier, len(around))
            moves = transfers(n)
            for move in moves[:6]:
                move.start()
            pack_x(n)
            for move in moves[6:]:
                move.start()
            sent += moves
            if n + 1 < steps:
                prepare(n + 1)
            for move in reversed(moves):
                move.wait_recv()
            unpack(n)
        last = n == steps - 1
        beyond = n % 2 == 0 and not last
        for t in range(tiles + 1 if beyond else tiles):
            cols = columns(t)
            if last:
                def emit(k, some, value):
                    out[k, :, cols] = value
            else:
                def emit(k, some, value):
                    adj[n + 1, k, t, pl.ds(0, some), :] = value
            advance(n, t, ring if beyond else width, emit)
            if last:
                store = pltpu.make_async_copy(out.at[:, :, cols], out_hbm.at[:, :, cols], out_sem.at[t])
                store.start()
                stores.append(store)
    store = pltpu.make_async_copy(sens, sens_hbm, out_sem.at[tiles])
    store.start()
    stores.append(store)
    for move in sent:
        move.wait_send()
    for store in stores:
        store.wait()


def solution(mesh):
    num_x, num_y = mesh.shape["gx"], mesh.shape["gy"]

    def body(saved_pops, seed_adjoint, solid_label, design_mask, design_field):
        steps = saved_pops.shape[0]
        width, flat = seed_adjoint.shape[1:]
        tiles = flat // LANES
        ring = width + EXTRA_ROWS
        pairs = (steps + 1) // 2
        fields = 3 * (steps // 2) + 2
        row_items = 19 + fields
        packs = (14 + fields + 1) // 2
        f32 = jnp.float32
        whole = pl.BlockSpec(memory_space=pltpu.HBM)
        return pl.pallas_call(
            functools.partial(kernel, num_x, num_y, steps, width, flat),
            out_shape=(
                jax.ShapeDtypeStruct((19, width, flat), f32),
                jax.ShapeDtypeStruct((width, flat), f32),
            ),
            in_specs=[whole] * 5,
            out_specs=(whole, whole),
            scratch_shapes=[
                pltpu.VMEM((steps, 19, width, flat), saved_pops.dtype),
                pltpu.VMEM((width, flat), jnp.int32),
                pltpu.VMEM((width, flat), jnp.int32),
                pltpu.VMEM((width, flat), f32),
                pltpu.VMEM((steps, 19, tiles + 1, ring, LANES), f32),
                pltpu.VMEM((pairs, 2, row_items * tiles, LANES), f32),
                pltpu.VMEM((pairs, 2, row_items * tiles, LANES), f32),
                pltpu.VMEM((pairs, 2, packs, ring, LANES), f32),
                pltpu.VMEM((pairs, 2, packs, ring, LANES), f32),
                pltpu.VMEM((steps, tiles, width, LANES), f32),
                pltpu.VMEM((steps, 3, tiles + 1, ring, LANES), f32),
                pltpu.VMEM((2, tiles + 1, ring, LANES), f32),
                pltpu.VMEM((19, width, flat), f32),
                pltpu.VMEM((width, flat), f32),
                pltpu.SemaphoreType.DMA((3,)),
                pltpu.SemaphoreType.DMA((tiles,)),
                pltpu.SemaphoreType.DMA((steps,)),
                pltpu.SemaphoreType.DMA((tiles + 1,)),
                pltpu.SemaphoreType.DMA((pairs, 8)),
                pltpu.SemaphoreType.DMA((pairs, 8)),
            ],
            compiler_params=pltpu.CompilerParams(
                collective_id=0, has_side_effects=True, vmem_limit_bytes=62 * 1024 * 1024
            ),
        )(saved_pops, seed_adjoint, solid_label, design_mask, design_field)

    in_specs = (
        P(None, None, "gx", "gy"),
        P(None, "gx", "gy"),
        P("gx", "gy"),
        P("gx", "gy"),
        P("gx", "gy"),
    )
    out_specs = (P(None, "gx", "gy"), P("gx", "gy"))
    return jax.shard_map(body, mesh=mesh, in_specs=in_specs, out_specs=out_specs, check_vma=False)
```

```python
import functools

import jax
import jax.numpy as jnp
import numpy as np
from jax import lax
from jax.experimental import pallas as pl
from jax.experimental.pallas import tpu as pltpu
from jax.sharding import PartitionSpec as P

NZ = 32
LANES = 128
MESH = pl.DeviceIdType.MESH

VELOCITIES = [
    (0, 0, 0),
    (1, 0, 0), (-1, 0, 0), (0, 1, 0), (0, -1, 0), (0, 0, 1), (0, 0, -1),
    (1, 1, 0), (1, -1, 0), (-1, 1, 0), (-1, -1, 0),
    (1, 0, 1), (1, 0, -1), (-1, 0, 1), (-1, 0, -1),
    (0, 1, 1), (0, 1, -1), (0, -1, 1), (0, -1, -1),
]
OPPOSITE = [0, 2, 1, 4, 3, 6, 5, 10, 9, 8, 7, 14, 13, 12, 11, 18, 17, 16, 15]
OMEGA_BASE = 1.0
OMEGA_SPAN = 0.8
SENS_SCALE = 10.0

EXTRA_ROWS = 8
WIDTH_SENT = 2


def roll_lanes(value, shift):
    shift = shift % LANES
    return value if shift == 0 else pltpu.roll(value, shift, 1)


def kernel(
    num_x, num_y, steps, width, flat,
    saved_hbm, seed_hbm, solid_hbm, mask_hbm, field_hbm,
    out_hbm, sens_hbm,
    saved, solid_ref, mask_ref, field_ref,
    adj, xsend, xrecv, ysend, yrecv, density_ref, speed, mark, out, sens,
    in_sem, seed_sem, saved_sem, out_sem, send_sem, recv_sem,
):
    tiles = flat // LANES
    ring = width + EXTRA_ROWS
    half = LANES // 2
    gx, gy = lax.axis_index("gx"), lax.axis_index("gy")
    west, east = lax.rem(gx + num_x - 1, num_x), lax.rem(gx + 1, num_x)
    south, north = lax.rem(gy + num_y - 1, num_y), lax.rem(gy + 1, num_y)

    barrier = pltpu.get_barrier_semaphore()
    around = [
        (west, south), (east, south), (west, north), (east, north),
        (west, gy), (east, gy), (gx, south), (gx, north),
    ]
    for device in around:
        pl.semaphore_signal(barrier, inc=1, device_id=device, device_id_type=MESH)
    own = pl.ds(0, width)

    def columns(t):
        return pl.ds(t * LANES, LANES)

    loads = [
        pltpu.make_async_copy(solid_hbm, solid_ref, in_sem.at[0]),
        pltpu.make_async_copy(mask_hbm, mask_ref, in_sem.at[1]),
        pltpu.make_async_copy(field_hbm, field_ref, in_sem.at[2]),
    ]
    seed_loads = [
        pltpu.make_async_copy(seed_hbm.at[:, :, columns(t)], adj.at[0, :, t, own], seed_sem.at[t])
        for t in range(tiles)
    ]
    saved_loads = [
        pltpu.make_async_copy(saved_hbm.at[steps - 1 - n], saved.at[steps - 1 - n], saved_sem.at[n])
        for n in range(steps)
    ]
    ahead = list(range(0, steps, 2))
    for n in ahead:
        saved_loads[n].start()
    for load in loads + seed_loads:
        load.start()
    for n in range(1, steps, 2):
        saved_loads[n].start()

    lane = lax.broadcasted_iota(jnp.int32, (ring, LANES), 1)
    depth = lane % NZ

    def view(n, item):
        if isinstance(item, int):
            return adj.at[n, item]
        return mark.at[item[1]] if item[0] == "mark" else speed.at[item[1], item[2]]

    def plan(n):
        fields = []
        if n == 0:
            fields = [("speed", m, axis) for m in ahead if m + 1 < steps for axis in range(3)]
            fields += [("mark", 0), ("mark", 1)]
        rows, packs = [], []
        for sign in (1, -1):
            near, next_one = (0, 1) if sign == 1 else (width - 1, width - 2)
            rows.append(
                [(k, near) for k in range(19) if VELOCITIES[k][0] * sign >= 0]
                + [(k, next_one) for k in range(19) if VELOCITIES[k][0] * sign > 0]
                + [(field, near) for field in fields]
            )
            packs.append([k for k in range(19) if VELOCITIES[k][1] * sign >= 0] + fields)
        return rows, packs

    def place(row):
        return width + row if row < WIDTH_SENT else ring - width + row

    def transfers(n):
        pair = n // 2
        rows, packs = plan(n)
        moves = []

        def add(src, dst, device):
            i = len(moves)
            moves.append(
                pltpu.make_async_remote_copy(
                    src_ref=src, dst_ref=dst,
                    send_sem=send_sem.at[pair, i], recv_sem=recv_sem.at[pair, i],
                    device_id=device, device_id_type=MESH,
                )
            )

        for side, by_x in ((0, (west, east)), (1, (west, east))):
            by_y = (south, north)[side]
            count = pl.ds(0, (len(packs[side]) + 1) // 2)
            for x, src_row, dst_row in (
                (by_x[0], 0, width), (by_x[1], width - WIDTH_SENT, ring - WIDTH_SENT),
            ):
                add(
                    ysend.at[pair, side, count, pl.ds(src_row, WIDTH_SENT)],
                    yrecv.at[pair, side, count, pl.ds(dst_row, WIDTH_SENT)],
                    (x, by_y),
                )
        for side, by_y in ((0, south), (1, north)):
            count = pl.ds(0, (len(packs[side]) + 1) // 2)
            add(ysend.at[pair, side, count, own], yrecv.at[pair, side, count, own], (gx, by_y))
        for side, by_x in ((0, west), (1, east)):
            count = pl.ds(0, len(rows[side]) * tiles)
            add(xsend.at[pair, side, count], xrecv.at[pair, side, count], (by_x, gy))
        return moves

    def first_half(side):
        return (lane < half) if side == 0 else (lane >= half)

    def pack_y(n, side):
        pack = plan(n)[1][side]
        t = 0 if side == 0 else tiles - 1
        for i in range(0, len(pack), 2):
            value = view(n, pack[i])[t, own, :]
            if i + 1 < len(pack):
                second = roll_lanes(view(n, pack[i + 1])[t, own, :], half)
                value = jnp.where(first_half(side)[:width], value, second)
            ysend[n // 2, side, i // 2, own, :] = value

    def pack_x(n):
        for side, rows in enumerate(plan(n)[0]):
            for j, (item, row) in enumerate(rows):
                for t in range(tiles):
                    xsend[n // 2, side, pl.ds(j * tiles + t, 1), :] = view(n, item)[t, pl.ds(row, 1), :]

    def unpack(n):
        rows, packs = plan(n)
        for side in range(2):
            for j, (item, row) in enumerate(rows[side]):
                for t in range(tiles):
                    view(n, item)[t, pl.ds(place(row), 1), :] = xrecv[
                        n // 2, side, pl.ds(j * tiles + t, 1), :
                    ]

        def arrived(side, item):
            if item not in packs[side]:
                return None
            i = packs[side].index(item)
            return roll_lanes(yrecv[n // 2, side, i // 2], half * (i % 2))

        for item in packs[0] + [item for item in packs[1] if item not in packs[0]]:
            after, before = arrived(0, item), arrived(1, item)
            if after is None or before is None:
                value = before if after is None else after
            else:
                value = jnp.where(lane < half, after, before)
            view(n, item)[tiles] = value

    def pulled_tile(n, k, t, count):
        step_x, step_y, step_z = VELOCITIES[k]
        if step_x == 0:
            rows = pl.ds(0, count)
        elif step_x == 1 and count == width:
            rows, step_x = pl.ds(1, count), 0
        else:
            rows = pl.ds(0, ring)
        value = adj[n, k, t, rows, :]
        if step_y != 0:
            beside = adj[n, k, (t + step_y) % (tiles + 1), rows, :]
            at = lane[: value.shape[0]]
            value = jnp.where(at < NZ if step_y == 1 else at >= LANES - NZ, beside, value)
        if step_x != 0:
            value = pltpu.roll(value, (-step_x) % ring, 0)[:count]
        shift = -NZ * step_y
        if step_z == 0:
            return roll_lanes(value, shift)
        return jnp.where(
            depth[:count] == (NZ - 1 if step_z == 1 else 0),
            roll_lanes(value, shift - step_z + NZ * step_z),
            roll_lanes(value, shift - step_z),
        )

    def moments(v):
        xy_a, xy_b, xy_c, xy_d = v(7) + v(8), v(9) + v(10), v(7) - v(8), v(9) - v(10)
        xz_a, xz_b, xz_c, xz_d = v(11) + v(12), v(13) + v(14), v(11) - v(12), v(13) - v(14)
        yz_a, yz_b, yz_c, yz_d = v(15) + v(16), v(17) + v(18), v(15) - v(16), v(17) - v(18)
        xy, xz, yz = xy_a + xy_b, xz_a + xz_b, yz_a + yz_b
        face_x, face_y, face_z = 2.0 * (v(1) + v(2)), 2.0 * (v(3) + v(4)), 2.0 * (v(5) + v(6))
        total = 12.0 * v(0) + (face_x + face_y + face_z) + (xy + xz + yz)
        first = (
            2.0 * (v(1) - v(2)) + (xy_a - xy_b) + (xz_a - xz_b),
            2.0 * (v(3) - v(4)) + (xy_c + xy_d) + (yz_a - yz_b),
            2.0 * (v(5) - v(6)) + (xz_c + xz_d) + (yz_c + yz_d),
        )
        second = (
            face_x + xy + xz, face_y + xy + yz, face_z + xz + yz,
            xy_c - xy_d, xz_c - xz_d, yz_c - yz_d,
        )
        return total, first, second

    def prepare(n):
        saved_loads[n].wait()
        for t in range(tiles):
            pops = [saved[steps - 1 - n, k, :, columns(t)].astype(jnp.float32) for k in range(19)]
            total, first, unused = moments(lambda k: pops[k])
            inverse = 1.0 / total
            density_ref[n, t] = total
            for axis in range(3):
                speed[n, axis, t, own, :] = first[axis] * inverse

    def advance(n, t, count, emit):
        s = steps - 1 - n
        cols = columns(t)
        rows = pl.ds(0, count)
        p = [pulled_tile(n, k, t, count) for k in range(19)]
        total, first, second = moments(lambda k: p[k])
        ux, uy, uz = (speed[n, axis, t, rows, :] for axis in range(3))
        xx, yy, zz, xy, xz, yz = (0.25 * value for value in second)
        gx_, gy_, gz_ = (value * (1.0 / 12.0) for value in first)
        total3 = total * (1.0 / 12.0)
        dx = gx_ + (xx - total3) * ux + xy * uy + xz * uz
        dy = gy_ + (yy - total3) * uy + xy * ux + yz * uz
        dz = gz_ + (zz - total3) * uz + xz * ux + yz * uy
        half_g = 0.5 * (gx_ * ux + gy_ * uy + gz_ * uz)
        half_d = 0.5 * (dx * ux + dy * uy + dz * uz)
        base = total * (1.0 / 36.0) + half_g
        solid = mark[1, t, rows, :] > 0.5
        if t < tiles:
            prod = [p[k][:width] * saved[s, k, :, cols].astype(jnp.float32) for k in range(19)]
            faces = (prod[1] + prod[2]) + (prod[3] + prod[4]) + (prod[5] + prod[6])
            edges = ((prod[7] + prod[8]) + (prod[9] + prod[10])) + (
                (prod[11] + prod[12]) + (prod[13] + prod[14])
            )
            edges = edges + ((prod[15] + prod[16]) + (prod[17] + prod[18]))
            gain = density_ref[n, t] * (base + half_d)[:width] - (12.0 * prod[0] + 2.0 * faces + edges)
            sens_now = gain if n == 0 else sens[:, cols] + gain
            if n == steps - 1:
                factor = mask_ref[:, cols].astype(jnp.float32) * (SENS_SCALE * OMEGA_SPAN / 36.0)
                sens_now = jnp.where(solid[:width], 0.0, factor * sens_now)
            sens[:, cols] = sens_now
        rate = mark[0, t, rows, :]
        keep = 1.0 - rate
        base = rate * (base - half_d)
        dx, dy, dz = rate * dx, rate * dy, rate * dz
        px, mx = base + dx, base - dx
        py, my = base + dy, base - dy
        terms = {
            (0, 0, 0): base,
            (1, 0, 0): px, (-1, 0, 0): mx, (0, 1, 0): py, (0, -1, 0): my,
            (0, 0, 1): base + dz, (0, 0, -1): base - dz,
            (1, 1, 0): px + dy, (1, -1, 0): px - dy, (-1, 1, 0): mx + dy, (-1, -1, 0): mx - dy,
            (1, 0, 1): px + dz, (1, 0, -1): px - dz, (-1, 0, 1): mx + dz, (-1, 0, -1): mx - dz,
            (0, 1, 1): py + dz, (0, 1, -1): py - dz, (0, -1, 1): my + dz, (0, -1, -1): my - dz,
        }
        for k in range(19):
            if t == tiles and VELOCITIES[k][1] == 0:
                continue
            some = count if VELOCITIES[k][0] != 0 else width
            emit(
                k, some,
                jnp.where(
                    solid[:some], p[OPPOSITE[k]][:some],
                    keep[:some] * p[k][:some] + terms[VELOCITIES[k]][:some],
                ),
            )

    for load in loads:
        load.wait()
    for t in range(tiles):
        cols = columns(t)
        mark[0, t, own, :] = (
            OMEGA_BASE + OMEGA_SPAN * field_ref[:, cols] * mask_ref[:, cols].astype(jnp.float32)
        )
        mark[1, t, own, :] = (solid_ref[:, cols] > 0).astype(jnp.float32)
    for n in ahead:
        prepare(n)
    for load in seed_loads:
        load.wait()

    sent, stores = [], []
    for n in range(steps):
        if n % 2 == 0:
            for side in range(2):
                pack_y(n, side)
            if n == 0:
                pl.semaphore_wait(barrier, len(around))
            moves = transfers(n)
            for move in moves[:6]:
                move.start()
            pack_x(n)
            for move in moves[6:]:
                move.start()
            sent += moves
            if n + 1 < steps:
                prepare(n + 1)
            for move in reversed(moves):
                move.wait_recv()
            unpack(n)
        last = n == steps - 1
        beyond = n % 2 == 0 and not last
        for t in range(tiles + 1 if beyond else tiles):
            cols = columns(t)
            if last:
                def emit(k, some, value):
                    out[k, :, cols] = value
            else:
                def emit(k, some, value):
                    adj[n + 1, k, t, pl.ds(0, some), :] = value
            advance(n, t, ring if beyond else width, emit)
            if last:
                store = pltpu.make_async_copy(out.at[:, :, cols], out_hbm.at[:, :, cols], out_sem.at[t])
                store.start()
                stores.append(store)
    store = pltpu.make_async_copy(sens, sens_hbm, out_sem.at[tiles])
    store.start()
    stores.append(store)
    for move in sent:
        move.wait_send()
    for store in stores:
        store.wait()


def hand_over(out_from, sens_from, out_to, sens_to, out, sens, in_sem, out_sem):
    parts = [(sens_from, sens, sens_to)]
    for first, last in ((0, 5), (5, 10), (10, 15), (15, 19)):
        part = pl.ds(first, last - first)
        parts.append((out_from.at[part], out.at[part], out_to.at[part]))
    loads = [pltpu.make_async_copy(a, b, in_sem.at[i]) for i, (a, b, c) in enumerate(parts)]
    stores = [pltpu.make_async_copy(b, c, out_sem.at[i]) for i, (a, b, c) in enumerate(parts)]
    for load in loads:
        load.start()
    for load, store in zip(loads, stores):
        load.wait()
        store.start()
    for store in stores:
        store.wait()


def solution(mesh):
    num_x, num_y = mesh.shape["gx"], mesh.shape["gy"]

    def body(saved_pops, seed_adjoint, solid_label, design_mask, design_field):
        steps = saved_pops.shape[0]
        width, flat = seed_adjoint.shape[1:]
        tiles = flat // LANES
        ring = width + EXTRA_ROWS
        pairs = (steps + 1) // 2
        fields = 3 * (steps // 2) + 2
        row_items = 19 + fields
        packs = (14 + fields + 1) // 2
        f32 = jnp.float32
        whole = pl.BlockSpec(memory_space=pltpu.HBM)
        results = pl.pallas_call(
            functools.partial(kernel, num_x, num_y, steps, width, flat),
            out_shape=(
                jax.ShapeDtypeStruct((19, width, flat), f32),
                jax.ShapeDtypeStruct((width, flat), f32),
            ),
            in_specs=[whole] * 5,
            out_specs=(whole, whole),
            scratch_shapes=[
                pltpu.VMEM((steps, 19, width, flat), saved_pops.dtype),
                pltpu.VMEM((width, flat), jnp.int32),
                pltpu.VMEM((width, flat), jnp.int32),
                pltpu.VMEM((width, flat), f32),
                pltpu.VMEM((steps, 19, tiles + 1, ring, LANES), f32),
                pltpu.VMEM((pairs, 2, row_items * tiles, LANES), f32),
                pltpu.VMEM((pairs, 2, row_items * tiles, LANES), f32),
                pltpu.VMEM((pairs, 2, packs, ring, LANES), f32),
                pltpu.VMEM((pairs, 2, packs, ring, LANES), f32),
                pltpu.VMEM((steps, tiles, width, LANES), f32),
                pltpu.VMEM((steps, 3, tiles + 1, ring, LANES), f32),
                pltpu.VMEM((2, tiles + 1, ring, LANES), f32),
                pltpu.VMEM((19, width, flat), f32),
                pltpu.VMEM((width, flat), f32),
                pltpu.SemaphoreType.DMA((3,)),
                pltpu.SemaphoreType.DMA((tiles,)),
                pltpu.SemaphoreType.DMA((steps,)),
                pltpu.SemaphoreType.DMA((tiles + 1,)),
                pltpu.SemaphoreType.DMA((pairs, 8)),
                pltpu.SemaphoreType.DMA((pairs, 8)),
            ],
            compiler_params=pltpu.CompilerParams(
                collective_id=0, has_side_effects=True, vmem_limit_bytes=62 * 1024 * 1024
            ),
        )(saved_pops, seed_adjoint, solid_label, design_mask, design_field)
        return pl.pallas_call(
            hand_over,
            out_shape=(
                jax.ShapeDtypeStruct((19, width, flat), f32),
                jax.ShapeDtypeStruct((width, flat), f32),
            ),
            in_specs=[whole] * 2,
            out_specs=(whole, whole),
            scratch_shapes=[
                pltpu.VMEM((19, width, flat), f32),
                pltpu.VMEM((width, flat), f32),
                pltpu.SemaphoreType.DMA((5,)),
                pltpu.SemaphoreType.DMA((5,)),
            ],
            compiler_params=pltpu.CompilerParams(vmem_limit_bytes=62 * 1024 * 1024),
        )(*results)

    in_specs = (
        P(None, None, "gx", "gy"),
        P(None, "gx", "gy"),
        P("gx", "gy"),
        P("gx", "gy"),
        P("gx", "gy"),
    )
    out_specs = (P(None, "gx", "gy"), P("gx", "gy"))
    return jax.shard_map(body, mesh=mesh, in_specs=in_specs, out_specs=out_specs, check_vma=False)
```
